32 devices in a mesh: seq: 8 (over z, x), head: 4 (over y, core).
Axes of the slice: x: 2, y: 2, z: 4, core: 2. Of those that a mesh axis runs over, the one named last changes fastest.
Arguments:
- queries: bfloat16 [2048, 2048], P('seq', 'head'), may hold values from -180 to 180
- keys: bfloat16 [2048, 2048], P('seq', 'head'), may hold values from -7 to 7
- values: bfloat16 [2048, 2048], P('seq', 'head'), may hold values from -6 to 6
- out_grad: bfloat16 [2048, 2048], P('seq', 'head'), may hold values from -6 to 6
- rand_blocks: int32 [32, 3], replicated, may hold values from 0 to 31, as said below
- glob_blocks: int32 [8], P('seq'), may hold values from 0 to 31, as said below
Outputs:
- attn_out: bfloat16 [2048, 2048], P('seq', 'head')
- query_grad: bfloat16 [2048, 2048], P('seq', 'head')
- key_grad: bfloat16 [2048, 2048], P('seq', 'head')
- value_grad: bfloat16 [2048, 2048], P('seq', 'head')
The draws below stay inside these ranges and needn't reach their ends.
Inputs may be any that keep to these rules, and one draw needn't show every extreme that they name: `rand_blocks`: rows 4 * i to 4 * (i + 1) - 1 are the query blocks of index i of seq. Among their 12 entries, the blocks of any one index j of seq (blocks 4 * j to 4 * (j + 1) - 1) are named at most 2 times; in every draw one index j is named exactly 2 times by the rows of every index i. `glob_blocks`: entry j is one of the blocks 4 * j to 4 * (j + 1) - 1.
All inputs are finite; a program needn't handle non-finite values.
Results may differ from the reference program's by a relative error of at most 0.0052.
Values may be sent and summed in bfloat16 or wider, within the bound.
A program may use at most 128 MiB of HBM per device.

```python
import math
import jax
import jax.numpy as jnp
from jax import lax

HDIM = 128
BLK = 64
GLEN = 16
R = 3
HEADS = 16
FEAT = 2048
BPD = 4
TOKENS = 2048
NBLK = 32
GTOK = 128
RCAP = 2
N_SEQ = 8


def pair_draw(key):
    base = jax.random.fold_in(key, 17)
    query_key, key_key = jax.random.split(base, 2)
    width = HEADS * HDIM
    queries = jax.random.truncated_normal(query_key, -6.0, 6.0, (TOKENS, width), jnp.float32)
    keys = jax.random.truncated_normal(key_key, -6.0, 6.0, (TOKENS, width), jnp.float32)
    return (queries, keys)


def draw_queries(key, part):
    return pair_draw(key)[0].astype(jnp.bfloat16)


def draw_keys(key, part):
    return pair_draw(key)[1].astype(jnp.bfloat16)


def draw_rand_blocks(key, part):
    base = jax.random.fold_in(key, 29)
    hot_key, perm_key, local_key = jax.random.split(base, 3)
    spots = BPD * R
    hot = jax.random.randint(hot_key, (), 0, N_SEQ).astype(jnp.int32)
    others = (hot + 1 + jnp.arange((N_SEQ - 1) * RCAP, dtype=jnp.int32) // RCAP) % N_SEQ

    def one_device(device_key):
        first_key, second_key = jax.random.split(device_key)
        mixed = jax.random.permutation(first_key, others)[:spots - RCAP]
        owners = jnp.concatenate([jnp.full((RCAP,), hot, jnp.int32), mixed.astype(jnp.int32)])
        return jax.random.permutation(second_key, owners)
    owners = jax.vmap(one_device)(jax.random.split(perm_key, N_SEQ))
    local = jax.random.randint(local_key, (N_SEQ, spots), 0, BPD).astype(jnp.int32)
    return (owners * BPD + local).reshape(NBLK, R).astype(jnp.int32)


def draw_glob_blocks(key, part):
    base = jax.random.fold_in(key, 41)
    device = jnp.arange(N_SEQ, dtype=jnp.int32)
    offset = jax.random.randint(base, (N_SEQ,), 0, BPD).astype(jnp.int32)
    return (device * BPD + offset).astype(jnp.int32)


def levels(key, dims, cuts, least, largest):
    loudness, own = 1.0, jax.random.fold_in(key, 6)
    for axis_at, parts in cuts:
        draws = jnp.exp(jax.random.uniform(jax.random.fold_in(own, axis_at), (parts,), jnp.float32, least / len(cuts), largest / len(cuts)))
        loudness = loudness * jnp.repeat(draws, dims[axis_at] // parts).reshape([-1 if axis == axis_at else 1 for axis in range(len(dims))])
    return loudness


def scatter_about(stream_key, extent, spread, limit, cuts=(), kind=jnp.bfloat16):
    array = spread * jax.random.normal(stream_key, extent, jnp.float32)
    if cuts:
        array = array * levels(stream_key, extent, cuts, -0.22, 0.18)
    return jnp.clip(array, -limit, limit).astype(kind)


def setup_inputs(seed: int = 0) -> dict:
    splits = jax.random.split(jax.random.key(seed), 7)
    return {
        "queries": draw_queries(jax.random.fold_in(splits[6], 71), 0),
        "keys": draw_keys(jax.random.fold_in(splits[6], 71), 0),
        "values": scatter_about(splits[2], (TOKENS, FEAT), 1.0, 6.0, ((0, 8), (1, 4))),
        "out_grad": scatter_about(splits[3], (TOKENS, FEAT), 1.0, 6.0, ((0, 8), (1, 4))),
        "rand_blocks": draw_rand_blocks(jax.random.fold_in(splits[6], 71), 0),
        "glob_blocks": draw_glob_blocks(jax.random.fold_in(splits[6], 71), 0),
    }


def add_block(accum, block_id, term):
    start = (block_id * BLK).astype(jnp.int32)
    old = lax.dynamic_slice_in_dim(accum, start, BLK, 0)
    return lax.dynamic_update_slice_in_dim(accum, old + term, start, 0)

def reference(queries, keys, values, out_grad, rand_blocks, glob_blocks):
    scale = 1.0 / math.sqrt(HDIM)
    width = HEADS * HDIM
    query_blocks = queries.reshape(NBLK, BLK, HEADS, HDIM)
    key_blocks = keys.reshape(NBLK, BLK, HEADS, HDIM)
    value_blocks = values.reshape(NBLK, BLK, HEADS, HDIM)
    grad_blocks = out_grad.reshape(NBLK, BLK, HEADS, HDIM)
    global_k = jnp.take(key_blocks, glob_blocks, axis=0)[:, :GLEN].reshape(GTOK, HEADS, HDIM)
    global_v = jnp.take(value_blocks, glob_blocks, axis=0)[:, :GLEN].reshape(GTOK, HEADS, HDIM)
    local_len = (3 + R) * BLK

    def step(carry, block_id):
        dk_accum, dv_accum, dk_global, dv_global = carry
        nearby = jnp.stack([block_id - 1, block_id, block_id + 1]).astype(jnp.int32)
        nearby_ok = (nearby >= 0) & (nearby < NBLK)
        nearby_safe = jnp.clip(nearby, 0, NBLK - 1).astype(jnp.int32)
        picks = rand_blocks[block_id].astype(jnp.int32)
        chosen = jnp.concatenate([nearby_safe, picks])
        local_k = jnp.take(key_blocks, chosen, axis=0).reshape(local_len, HEADS, HDIM)
        local_v = jnp.take(value_blocks, chosen, axis=0).reshape(local_len, HEADS, HDIM)
        all_k = jnp.concatenate([local_k, global_k], 0).astype(jnp.float32)
        all_v = jnp.concatenate([local_v, global_v], 0).astype(jnp.float32)
        visible = jnp.concatenate([jnp.repeat(nearby_ok, BLK), jnp.ones((R * BLK + GTOK,), bool)])
        query_now = query_blocks[block_id].astype(jnp.float32)
        grad_now = grad_blocks[block_id].astype(jnp.float32)
        scores = jnp.einsum('qhd,khd->hqk', query_now, all_k) * scale
        scores = jnp.where(visible[None, None, :], scores, -jnp.inf)
        top = lax.optimization_barrier(jnp.max(scores, axis=-1, keepdims=True))
        expo = jnp.exp(scores - top)
        probs = expo / lax.optimization_barrier(jnp.sum(expo, axis=-1, keepdims=True))
        probs_b = probs.astype(jnp.bfloat16)
        out_now = jnp.einsum('hqk,khd->qhd', probs_b.astype(jnp.float32), all_v).astype(jnp.bfloat16)
        dprobs = jnp.einsum('qhd,khd->hqk', grad_now, all_v)
        delta = lax.optimization_barrier(jnp.sum(probs * dprobs, axis=-1, keepdims=True))
        dscores = (probs * (dprobs - delta) * scale).astype(jnp.bfloat16)
        dq_now = jnp.einsum('hqk,khd->qhd', dscores.astype(jnp.float32), all_k).astype(jnp.bfloat16)
        dk_terms = jnp.einsum('hqk,qhd->khd', dscores.astype(jnp.float32), query_now).reshape(-1, width)
        dv_terms = jnp.einsum('hqk,qhd->khd', probs_b.astype(jnp.float32), grad_now).reshape(-1, width)
        for which in range(3):
            keep = nearby_ok[which].astype(jnp.float32)
            dk_accum = add_block(dk_accum, nearby_safe[which], dk_terms[which * BLK:(which + 1) * BLK] * keep)
            dv_accum = add_block(dv_accum, nearby_safe[which], dv_terms[which * BLK:(which + 1) * BLK] * keep)
        for which in range(R):
            lower = (3 + which) * BLK
            dk_round = lax.optimization_barrier(dk_terms[lower:lower + BLK].astype(jnp.bfloat16)).astype(jnp.float32)
            dv_round = lax.optimization_barrier(dv_terms[lower:lower + BLK].astype(jnp.bfloat16)).astype(jnp.float32)
            dk_accum = add_block(dk_accum, picks[which], dk_round)
            dv_accum = add_block(dv_accum, picks[which], dv_round)
        dk_global = dk_global + dk_terms[local_len:]
        dv_global = dv_global + dv_terms[local_len:]
        outputs = (out_now.reshape(BLK, width), dq_now.reshape(BLK, width))
        return ((dk_accum, dv_accum, dk_global, dv_global), outputs)
    start_carry = (jnp.zeros((TOKENS, width), jnp.float32), jnp.zeros((TOKENS, width), jnp.float32), jnp.zeros((GTOK, width), jnp.float32), jnp.zeros((GTOK, width), jnp.float32))
    final, stacked = lax.scan(step, start_carry, jnp.arange(NBLK, dtype=jnp.int32))
    dk_accum, dv_accum, dk_global, dv_global = final
    dk_full = dk_accum.reshape(NBLK, BLK, width).at[glob_blocks, :GLEN].add(dk_global.reshape(N_SEQ, GLEN, width))
    dv_full = dv_accum.reshape(NBLK, BLK, width).at[glob_blocks, :GLEN].add(dv_global.reshape(N_SEQ, GLEN, width))
    attn_out = stacked[0].reshape(TOKENS, width)
    query_grad = stacked[1].reshape(TOKENS, width)
    key_grad = dk_full.reshape(TOKENS, width).astype(jnp.bfloat16)
    value_grad = dv_full.reshape(TOKENS, width).astype(jnp.bfloat16)
    return (attn_out, query_grad, key_grad, value_grad)
```

```python
import functools
import math

import jax
import jax.numpy as jnp
from jax import lax
from jax.experimental import pallas as pl
from jax.experimental.pallas import tpu as pltpu
from jax.sharding import PartitionSpec as P

HDIM = 128
BLK = 64
GLEN = 16
MESH = pl.DeviceIdType.MESH
F32 = jnp.float32
BF16 = jnp.bfloat16


def dot(a, b, dims):
    return lax.dot_general(a, b, (dims, ((), ())), preferred_element_type=F32)


def kernel(
    nz, nx, nb, per, cap, heads,
    rb_ref, gb_ref, q_ref, k_ref, v_ref, g_ref,
    o_ref, dq_ref, dk_ref, dv_ref,
    col, xs, xr, yr, hr, wh, wr, rin, rout, wacc, gath, gkv, tmp, tr, gacc,
    tgt, inv, place,
    z_send, z_recv, x_send, x_recv, y_send, y_recv, h_send, h_recv, w_send, w_recv, r_send, r_recv,
):
    n = nz * nx
    rows = nb * BLK
    spots = nb * per
    ext = rows + GLEN
    scale = 1.0 / math.sqrt(HDIM)
    me = lax.axis_index("seq")
    z = me // nx
    x = me % nx

    def lanes(h):
        return pl.ds(pl.multiple_of(h * HDIM, HDIM), HDIM)

    def remote(src, dst, send, recv, dev):
        return pltpu.make_async_remote_copy(
            src_ref=src, dst_ref=dst, send_sem=send, recv_sem=recv,
            device_id={"seq": dev}, device_id_type=MESH,
        )

    barrier = pltpu.get_barrier_semaphore()
    for step in range(1, n):
        pl.semaphore_signal(
            barrier, inc=1, device_id={"seq": lax.rem(me + step, n)}, device_id_type=MESH
        )
    own_global = gb_ref[0] - me * nb

    def pack_own(h, _):
        for kv, ref in enumerate((k_ref, v_ref)):
            col[h, z, kv, 0:rows, :] = ref[:, lanes(h)]
            picked = ref[0:GLEN, lanes(h)]
            for blk in range(1, nb):
                at = slice(blk * BLK, blk * BLK + GLEN)
                picked = jnp.where(own_global == blk, ref[at, lanes(h)], picked)
            col[h, z, kv, rows:ext, :] = picked
        return 0

    lax.fori_loop(0, heads, pack_own, 0)
    pl.semaphore_wait(barrier, n - 1)

    def z_copy(h, zz, up):
        dev = me + (nx if up else -nx)
        return remote(
            col.at[h, zz], col.at[h, zz], z_send.at[h, zz, int(up)], z_recv.at[h, zz], dev
        )

    def halo_copy(h, nxt):
        edge = pl.ds(rows - BLK, BLK) if nxt else pl.ds(0, BLK)
        slot = 0 if nxt else 1
        return remote(
            col.at[h, z, :, edge, :], hr.at[h, slot],
            h_send.at[h, slot], h_recv.at[h, slot], me + (1 if nxt else -1),
        )

    def first_sends(h, _):
        @pl.when(z < nz - 1)
        def _():
            z_copy(h, z, True).start()

        @pl.when(z > 0)
        def _():
            z_copy(h, z, False).start()

        @pl.when(me < n - 1)
        def _():
            halo_copy(h, True).start()

        @pl.when(me > 0)
        def _():
            halo_copy(h, False).start()

        return 0

    lax.fori_loop(0, heads, first_sends, 0)

    @pl.when(me == 0)
    def _():
        hr[:, 0] = jnp.zeros_like(hr[:, 0])

    @pl.when(me == n - 1)
    def _():
        hr[:, 1] = jnp.zeros_like(hr[:, 1])

    def own_entry(t):
        return rb_ref[me * nb + t // per, t % per]

    for t in range(spots):
        owner = lax.div(own_entry(t), nb)
        rank = jnp.int32(0)
        for s in range(t):
            rank = rank + (lax.div(own_entry(s), nb) == owner).astype(jnp.int32)
        place[t] = owner * cap + rank

    def fill_inv(j, _):
        count = jnp.int32(0)
        found = [jnp.int32(spots)] * cap
        for t in range(spots):
            hit = lax.div(own_entry(t), nb) == j
            for c in range(cap):
                found[c] = jnp.where(hit & (count == c), jnp.int32(t), found[c])
            count = count + hit.astype(jnp.int32)
        for c in range(cap):
            inv[j * cap + c] = found[c]
        return 0

    lax.fori_loop(0, n, fill_inv, 0)

    def fill_tgt(at, _):
        px = at // nz
        zz = at % nz
        j = zz * nx + x
        count = jnp.int32(0)
        found = [jnp.int32(-1)] * cap
        for t in range(spots):
            block = rb_ref[(z * nx + px) * nb + t // per, t % per]
            hit = lax.div(block, nb) == j
            for c in range(cap):
                found[c] = jnp.where(hit & (count == c), block - j * nb, found[c])
            count = count + hit.astype(jnp.int32)
        for c in range(cap):
            tgt[at * cap + c] = found[c]
        return 0

    lax.fori_loop(0, nx * nz, fill_tgt, 0)
    tr[spots] = jnp.zeros_like(tr[spots])

    def x_copy(h, px, zz):
        return remote(
            xs.at[h, px, zz], xr.at[h, x, zz], x_send.at[h, px, zz], x_recv.at[h, x, zz],
            z * nx + px,
        )

    def x_wait(h, xo, zz):
        remote(
            xs.at[h, xo, zz], xr.at[h, xo, zz], x_send.at[h, xo, zz], x_recv.at[h, xo, zz],
            z * nx + xo,
        ).wait_recv()

    def y_copy(h, xo, zz):
        return remote(
            xs.at[h, xo, zz], yr.at[h, x, zz], y_send.at[h, xo, zz], y_recv.at[h, x, zz],
            z * nx + xo,
        )

    def y_wait(h, d, zz):
        remote(
            xs.at[h, d, zz], yr.at[h, d, zz], y_send.at[h, d, zz], y_recv.at[h, d, zz],
            z * nx + d,
        ).wait_recv()

    def serve(h, zz):
        for blk in range(nb):
            tmp[blk] = col[h, zz, :, blk * BLK : (blk + 1) * BLK, :]

        def one(px, _):
            def put(dst):
                for c in range(cap):
                    block = jnp.maximum(tgt[(px * nz + zz) * cap + c], 0)
                    dst[h, px, zz, :, c * BLK : (c + 1) * BLK, :] = tmp[block]
                dst[h, px, zz, :, cap * BLK :, :] = col[h, zz, :, rows:ext, :]

            @pl.when(px == x)
            def _():
                put(xr)

            @pl.when(px != x)
            def _():
                put(xs)
                x_copy(h, px, zz).start()

            return 0

        lax.fori_loop(0, nx, one, 0)

    def gather_stage(h):
        serve(h, z)

        def one(s, _):
            @pl.when(z - s >= 0)
            def _():
                zz = z - s
                z_copy(h, zz, True).wait_recv()

                @pl.when(z < nz - 1)
                def _():
                    z_copy(h, zz, True).start()

                serve(h, zz)

            @pl.when(z + s < nz)
            def _():
                zz = z + s
                z_copy(h, zz, False).wait_recv()

                @pl.when(z > 0)
                def _():
                    z_copy(h, zz, False).start()

                serve(h, zz)

            return 0

        lax.fori_loop(1, nz, one, 0)

    def w_copy(h, nxt):
        slot = 1 if nxt else 0
        return remote(
            wh.at[h, slot], wr.at[h, slot], w_send.at[h, slot], w_recv.at[h, slot],
            me + (1 if nxt else -1),
        )

    def compute_stage(h):
        def collect(j, _):
            zz = j // nx
            xo = j % nx

            @pl.when(xo != x)
            def _():
                x_wait(h, xo, zz)

            for c in range(cap):
                gath[j * cap + c] = xr[h, xo, zz, :, c * BLK : (c + 1) * BLK, :]
            gkv[:, pl.ds(pl.multiple_of(j * GLEN, GLEN), GLEN), :] = xr[h, xo, zz, :, cap * BLK :, :]
            return 0

        lax.fori_loop(0, n, collect, 0)

        @pl.when(me > 0)
        def _():
            halo_copy(h, True).wait_recv()

        @pl.when(me < n - 1)
        def _():
            halo_copy(h, False).wait_recv()

        def window(blk):
            if blk < 0:
                return hr[h, 0]
            if blk >= nb:
                return hr[h, 1]
            return col[h, z, :, blk * BLK : (blk + 1) * BLK, :]

        wacc[h] = jnp.zeros_like(wacc[h])
        length = (3 + per) * BLK + n * GLEN
        column = lax.broadcasted_iota(jnp.int32, (BLK, length), 1)
        low = (3 + per) * BLK
        gsum_k = gsum_v = None
        for b in range(nb):
            parts = [window(b - 1), window(b), window(b + 1)]
            parts += [gath[place[b * per + r]] for r in range(per)]
            parts.append(gkv[...])
            kcat = jnp.concatenate([p[0] for p in parts], 0)
            vcat = jnp.concatenate([p[1] for p in parts], 0)
            at = slice(b * BLK, (b + 1) * BLK)
            q = q_ref[at, lanes(h)]
            g = g_ref[at, lanes(h)]
            s = dot(q, kcat, ((1,), (1,))) * scale
            if b == 0:
                s = jnp.where((column < BLK) & (me == 0), -jnp.inf, s)
            if b == nb - 1:
                s = jnp.where(
                    (column >= 2 * BLK) & (column < 3 * BLK) & (me == n - 1), -jnp.inf, s
                )
            e = jnp.exp(s - jnp.max(s, axis=1, keepdims=True))
            p = e * (1.0 / jnp.sum(e, axis=1, keepdims=True))
            pb = p.astype(BF16)
            o_ref[at, lanes(h)] = dot(pb, vcat, ((1,), (0,))).astype(BF16)
            dp = dot(g, vcat, ((1,), (1,)))
            delta = jnp.sum(p * dp, axis=1, keepdims=True)
            ds = (p * (dp - delta) * scale).astype(BF16)
            dq_ref[at, lanes(h)] = dot(ds, kcat, ((1,), (0,))).astype(BF16)
            dk = dot(ds, q, ((0,), (0,)))
            dv = dot(pb, g, ((0,), (0,)))
            for kv, term in ((0, dk), (1, dv)):
                wacc[h, kv, b * BLK : (b + 3) * BLK, :] += term[: 3 * BLK]
                for r in range(per):
                    tr[b * per + r, kv] = term[(3 + r) * BLK : (4 + r) * BLK].astype(BF16)
            gsum_k = dk[low:] if b == 0 else gsum_k + dk[low:]
            gsum_v = dv[low:] if b == 0 else gsum_v + dv[low:]
        gacc[0] = gsum_k.astype(BF16)
        gacc[1] = gsum_v.astype(BF16)

        def give(j, _):
            zz = j // nx
            xo = j % nx

            def put(dst):
                for c in range(cap):
                    dst[h, xo, zz, :, c * BLK : (c + 1) * BLK, :] = tr[inv[j * cap + c]]
                dst[h, xo, zz, :, cap * BLK :, :] = gacc[
                    :, pl.ds(pl.multiple_of(j * GLEN, GLEN), GLEN), :
                ]

            @pl.when(xo == x)
            def _():
                put(yr)

            @pl.when(xo != x)
            def _():
                x_copy(h, xo, zz).wait_send()
                put(xs)
                y_copy(h, xo, zz).start()

            return 0

        lax.fori_loop(0, n, give, 0)

        @pl.when(me > 0)
        def _():
            wh[h, 0] = wacc[h, :, 0:BLK, :].astype(BF16)
            w_copy(h, False).start()

        @pl.when(me < n - 1)
        def _():
            wh[h, 1] = wacc[h, :, rows + BLK :, :].astype(BF16)
            w_copy(h, True).start()

    def column_terms(h, zz):
        pieces = []
        slots = [
            (tgt[(d * nz + zz) * cap + c], yr[h, d, zz, :, c * BLK : (c + 1) * BLK, :].astype(F32))
            for d in range(nx)
            for c in range(cap)
        ]
        for blk in range(nb):
            total = None
            for target, term in slots:
                part = jnp.where(target == blk, term, 0.0)
                total = part if total is None else total + part
            pieces.append(total)
        total = None
        for d in range(nx):
            part = yr[h, d, zz, :, cap * BLK :, :].astype(F32)
            total = part if total is None else total + part
        return pieces, total

    def r_copy(h, zz, slot, up):
        return remote(
            rout.at[h, zz], rin.at[h, slot], r_send.at[h, zz], r_recv.at[h, slot],
            me + (nx if up else -nx),
        )

    def pass_on(h, zz, more):
        pieces, glob = column_terms(h, zz)

        def put(extra):
            for blk in range(nb):
                at = slice(blk * BLK, (blk + 1) * BLK)
                rout[h, zz, :, at, :] = extra(pieces[blk], at).astype(BF16)
            rout[h, zz, :, rows:ext, :] = extra(glob, slice(rows, ext)).astype(BF16)

        @pl.when(more)
        def _():
            r_copy(h, zz, zz, False).wait_recv()
            put(lambda v, at: v + rin[h, zz, :, at, :].astype(F32))

        @pl.when(jnp.logical_not(more))
        def _():
            put(lambda v, at: v)

    def return_stage(h):
        def arrive(at, _):
            d = at // nz

            @pl.when(d != x)
            def _():
                y_wait(h, d, at % nz)

            return 0

        lax.fori_loop(0, nx * nz, arrive, 0)

        def one(i, _):
            down = i
            up = nz - 1 - i

            @pl.when(down < z)
            def _():
                pass_on(h, down, z < nz - 1)
                r_copy(h, down, down, False).start()

            @pl.when(up > z)
            def _():
                pass_on(h, up, z > 0)

                @pl.when(up == z + 1)
                def _():
                    r_copy(h, up, nz, True).start()

                @pl.when(up != z + 1)
                def _():
                    r_copy(h, up, up, True).start()

            return 0

        lax.fori_loop(0, nz - 1, one, 0)

        pieces, glob = column_terms(h, z)
        for blk in range(nb):
            at = slice(blk * BLK, (blk + 1) * BLK)
            wacc[h, :, BLK + blk * BLK : 2 * BLK + blk * BLK, :] += pieces[blk]

        @pl.when(me > 0)
        def _():
            w_copy(h, True).wait_recv()
            wacc[h, :, BLK : 2 * BLK, :] += wr[h, 1].astype(F32)

        @pl.when(me < n - 1)
        def _():
            w_copy(h, False).wait_recv()
            wacc[h, :, rows : rows + BLK, :] += wr[h, 0].astype(F32)

        @pl.when(z == nz - 1)
        def _():
            rin[h, z] = jnp.zeros_like(rin[h, z])

        @pl.when(z < nz - 1)
        def _():
            r_copy(h, z, z, False).wait_recv()

        @pl.when(z == 0)
        def _():
            rin[h, nz] = jnp.zeros_like(rin[h, nz])

        @pl.when(z > 0)
        def _():
            r_copy(h, z, nz, True).wait_recv()

        glob = glob + rin[h, z, :, rows:ext, :].astype(F32) + rin[h, nz, :, rows:ext, :].astype(F32)
        for blk in range(nb):
            at = slice(blk * BLK, (blk + 1) * BLK)
            total = (
                wacc[h, :, BLK + blk * BLK : 2 * BLK + blk * BLK, :]
                + rin[h, z, :, at, :].astype(F32)
                + rin[h, nz, :, at, :].astype(F32)
            )
            top = total[:, :GLEN] + jnp.where(own_global == blk, glob, 0.0)
            total = jnp.concatenate([top, total[:, GLEN:]], 1).astype(BF16)
            dk_ref[at, lanes(h)] = total[0]
            dv_ref[at, lanes(h)] = total[1]

    def turn(t, _):
        @pl.when(t < heads)
        def _():
            gather_stage(t)

        @pl.when((t >= 1) & (t <= heads))
        def _():
            compute_stage(t - 1)

        @pl.when(t >= 2)
        def _():
            return_stage(t - 2)

        return 0

    lax.fori_loop(0, heads + 2, turn, 0)

    def drain(h, _):
        def shard(zz, _):
            @pl.when((zz <= z) & (z < nz - 1))
            def _():
                z_copy(h, zz, True).wait_send()

            @pl.when((zz >= z) & (z > 0))
            def _():
                z_copy(h, zz, False).wait_send()

            @pl.when(zz != z)
            def _():
                r_copy(h, zz, zz, False).wait_send()

            def partner(px, _):
                @pl.when(px != x)
                def _():
                    y_copy(h, px, zz).wait_send()

                return 0

            lax.fori_loop(0, nx, partner, 0)
            return 0

        lax.fori_loop(0, nz, shard, 0)

        @pl.when(me < n - 1)
        def _():
            halo_copy(h, True).wait_send()
            w_copy(h, True).wait_send()

        @pl.when(me > 0)
        def _():
            halo_copy(h, False).wait_send()
            w_copy(h, False).wait_send()

        return 0

    lax.fori_loop(0, heads, drain, 0)


def grid_of(n):
    nx = 1
    while nx * nx * 4 <= n and n % (nx * 2) == 0:
        nx *= 2
    return n // nx, nx


def shards(n, queries, keys, values, out_grad, rand_blocks, glob_blocks):
    rows, width = queries.shape
    heads = width // HDIM
    nb = rows // BLK
    per = rand_blocks.shape[1]
    spots = nb * per
    cap = max(2, (spots + n - 1) // n)
    nz, nx = grid_of(n)
    ext = rows + GLEN
    xrows = cap * BLK + GLEN
    out = jax.ShapeDtypeStruct((rows, width), BF16)
    vmem = pl.BlockSpec(memory_space=pltpu.VMEM)
    smem = pl.BlockSpec(memory_space=pltpu.SMEM)
    dma = pltpu.SemaphoreType.DMA
    slots = pltpu.VMEM((heads, nx, nz, 2, xrows, HDIM), BF16)
    edges = pltpu.VMEM((heads, 2, 2, BLK, HDIM), BF16)
    return pl.pallas_call(
        functools.partial(kernel, nz, nx, nb, per, cap, heads),
        out_shape=[out] * 4,
        in_specs=[smem, smem, vmem, vmem, vmem, vmem],
        out_specs=[vmem] * 4,
        scratch_shapes=[
            pltpu.VMEM((heads, nz, 2, ext, HDIM), BF16),
            slots, slots, slots,
            edges, edges, edges,
            pltpu.VMEM((heads, nz + 1, 2, ext, HDIM), BF16),
            pltpu.VMEM((heads, nz, 2, ext, HDIM), BF16),
            pltpu.VMEM((heads, 2, rows + 2 * BLK, HDIM), F32),
            pltpu.VMEM((n * cap, 2, BLK, HDIM), BF16),
            pltpu.VMEM((2, n * GLEN, HDIM), BF16),
            pltpu.VMEM((nb, 2, BLK, HDIM), BF16),
            pltpu.VMEM((spots + 1, 2, BLK, HDIM), BF16),
            pltpu.VMEM((2, n * GLEN, HDIM), BF16),
            pltpu.SMEM((nx * nz * cap,), jnp.int32),
            pltpu.SMEM((n * cap,), jnp.int32),
            pltpu.SMEM((spots,), jnp.int32),
            dma((heads, nz, 2)), dma((heads, nz)),
            dma((heads, nx, nz)), dma((heads, nx, nz)),
            dma((heads, nx, nz)), dma((heads, nx, nz)),
            dma((heads, 2)), dma((heads, 2)),
            dma((heads, 2)), dma((heads, 2)),
            dma((heads, nz)), dma((heads, nz + 1)),
        ],
        compiler_params=pltpu.CompilerParams(
            collective_id=0, has_side_effects=True, vmem_limit_bytes=60 * 1024 * 1024
        ),
    )(rand_blocks, glob_blocks, queries, keys, values, out_grad)


def solution(mesh):
    split = P("seq", "head")
    return jax.shard_map(
        functools.partial(shards, mesh.shape["seq"]),
        mesh=mesh,
        in_specs=(split, split, split, split, P(), P("seq")),
        out_specs=(split, split, split, split),
        check_vma=False,
    )
```

```python
import functools
import math

import jax
import jax.numpy as jnp
from jax import lax
from jax.experimental import pallas as pl
from jax.experimental.pallas import tpu as pltpu
from jax.sharding import PartitionSpec as P

HDIM = 128
BLK = 64
GLEN = 16
MESH = pl.DeviceIdType.MESH
F32 = jnp.float32
BF16 = jnp.bfloat16


def dot(a, b, dims):
    return lax.dot_general(a, b, (dims, ((), ())), preferred_element_type=F32)


def kernel(
    nz, nx, nb, per, cap, heads,
    rb_ref, gb_ref, q_ref, k_ref, v_ref, g_ref,
    o_ref, dq_ref, dk_ref, dv_ref,
    col, xs, xr, yr, hr, wh, wr, rin, rout, wacc, gath, gkv, tmp, tr, gacc,
    tgt, inv, place,
    z_send, z_recv, x_send, x_recv, y_send, y_recv, h_send, h_recv, w_send, w_recv, r_send, r_recv,
):
    n = nz * nx
    rows = nb * BLK
    spots = nb * per
    ext = rows + GLEN
    scale = 1.0 / math.sqrt(HDIM)
    lead = 2
    me = lax.axis_index("seq")
    z = me // nx
    x = me % nx

    def lanes(h):
        return pl.ds(pl.multiple_of(h * HDIM, HDIM), HDIM)

    def remote(src, dst, send, recv, dev):
        return pltpu.make_async_remote_copy(
            src_ref=src, dst_ref=dst, send_sem=send, recv_sem=recv,
            device_id={"seq": dev}, device_id_type=MESH,
        )

    barrier = pltpu.get_barrier_semaphore()
    for step in range(1, n):
        pl.semaphore_signal(
            barrier, inc=1, device_id={"seq": lax.rem(me + step, n)}, device_id_type=MESH
        )
    own_global = gb_ref[0] - me * nb

    def pack_own(h, _):
        for kv, ref in enumerate((k_ref, v_ref)):
            col[h, z, kv, 0:rows, :] = ref[:, lanes(h)]
            picked = ref[0:GLEN, lanes(h)]
            for blk in range(1, nb):
                at = slice(blk * BLK, blk * BLK + GLEN)
                picked = jnp.where(own_global == blk, ref[at, lanes(h)], picked)
            col[h, z, kv, rows:ext, :] = picked
        return 0

    lax.fori_loop(0, heads, pack_own, 0)
    pl.semaphore_wait(barrier, n - 1)

    def z_copy(h, zz, up):
        dev = me + (nx if up else -nx)
        return remote(
            col.at[h, zz], col.at[h, zz], z_send.at[h, zz, int(up)], z_recv.at[h, zz], dev
        )

    def halo_copy(h, nxt):
        edge = pl.ds(rows - BLK, BLK) if nxt else pl.ds(0, BLK)
        slot = 0 if nxt else 1
        return remote(
            col.at[h, z, :, edge, :], hr.at[h, slot],
            h_send.at[h, slot], h_recv.at[h, slot], me + (1 if nxt else -1),
        )

    def first_sends(h, _):
        @pl.when(z < nz - 1)
        def _():
            z_copy(h, z, True).start()

        @pl.when(z > 0)
        def _():
            z_copy(h, z, False).start()

        @pl.when(me < n - 1)
        def _():
            halo_copy(h, True).start()

        @pl.when(me > 0)
        def _():
            halo_copy(h, False).start()

        return 0

    lax.fori_loop(0, min(lead, heads), first_sends, 0)

    @pl.when(me == 0)
    def _():
        hr[:, 0] = jnp.zeros_like(hr[:, 0])

    @pl.when(me == n - 1)
    def _():
        hr[:, 1] = jnp.zeros_like(hr[:, 1])

    def own_entry(t):
        return rb_ref[me * nb + t // per, t % per]

    for t in range(spots):
        owner = lax.div(own_entry(t), nb)
        rank = jnp.int32(0)
        for s in range(t):
            rank = rank + (lax.div(own_entry(s), nb) == owner).astype(jnp.int32)
        place[t] = owner * cap + rank

    def fill_inv(j, _):
        count = jnp.int32(0)
        found = [jnp.int32(spots)] * cap
        for t in range(spots):
            hit = lax.div(own_entry(t), nb) == j
            for c in range(cap):
                found[c] = jnp.where(hit & (count == c), jnp.int32(t), found[c])
            count = count + hit.astype(jnp.int32)
        for c in range(cap):
            inv[j * cap + c] = found[c]
        return 0

    lax.fori_loop(0, n, fill_inv, 0)

    def fill_tgt(at, _):
        px = at // nz
        zz = at % nz
        j = zz * nx + x
        count = jnp.int32(0)
        found = [jnp.int32(-1)] * cap
        for t in range(spots):
            block = rb_ref[(z * nx + px) * nb + t // per, t % per]
            hit = lax.div(block, nb) == j
            for c in range(cap):
                found[c] = jnp.where(hit & (count == c), block - j * nb, found[c])
            count = count + hit.astype(jnp.int32)
        for c in range(cap):
            tgt[at * cap + c] = found[c]
        return 0

    lax.fori_loop(0, nx * nz, fill_tgt, 0)
    tr[spots] = jnp.zeros_like(tr[spots])

    def x_copy(h, px, zz):
        return remote(
            xs.at[h, px, zz], xr.at[h, x, zz], x_send.at[h, px, zz], x_recv.at[h, x, zz],
            z * nx + px,
        )

    def x_wait(h, xo, zz):
        remote(
            xs.at[h, xo, zz], xr.at[h, xo, zz], x_send.at[h, xo, zz], x_recv.at[h, xo, zz],
            z * nx + xo,
        ).wait_recv()

    def y_copy(h, xo, zz):
        return remote(
            xs.at[h, xo, zz], yr.at[h, x, zz], y_send.at[h, xo, zz], y_recv.at[h, x, zz],
            z * nx + xo,
        )

    def y_wait(h, d, zz):
        remote(
            xs.at[h, d, zz], yr.at[h, d, zz], y_send.at[h, d, zz], y_recv.at[h, d, zz],
            z * nx + d,
        ).wait_recv()

    def serve(h, zz):
        for blk in range(nb):
            tmp[blk] = col[h, zz, :, blk * BLK : (blk + 1) * BLK, :]

        def one(px, _):
            def put(dst):
                for c in range(cap):
                    block = jnp.maximum(tgt[(px * nz + zz) * cap + c], 0)
                    dst[h, px, zz, :, c * BLK : (c + 1) * BLK, :] = tmp[block]
                dst[h, px, zz, :, cap * BLK :, :] = col[h, zz, :, rows:ext, :]

            @pl.when(px == x)
            def _():
                put(xr)

            @pl.when(px != x)
            def _():
                put(xs)
                x_copy(h, px, zz).start()

            return 0

        lax.fori_loop(0, nx, one, 0)

    def gather_stage(t):
        def one(s, _):
            h = t + nz - 1 - s

            @pl.when((h >= 0) & (h < heads) & (s == 1))
            def _():
                @pl.when(h + lead < heads)
                def _():
                    first_sends(h + lead, 0)

                serve(h, z)

            @pl.when((h >= 0) & (h < heads) & (z - s >= 0))
            def _():
                zz = z - s
                z_copy(h, zz, True).wait_recv()

                @pl.when(z < nz - 1)
                def _():
                    z_copy(h, zz, True).start()

                serve(h, zz)

            @pl.when((h >= 0) & (h < heads) & (z + s < nz))
            def _():
                zz = z + s
                z_copy(h, zz, False).wait_recv()

                @pl.when(z > 0)
                def _():
                    z_copy(h, zz, False).start()

                serve(h, zz)

            return 0

        lax.fori_loop(1, nz, one, 0)

    def w_copy(h, nxt):
        slot = 1 if nxt else 0
        return remote(
            wh.at[h, slot], wr.at[h, slot], w_send.at[h, slot], w_recv.at[h, slot],
            me + (1 if nxt else -1),
        )

    def compute_stage(h):
        def collect(j, _):
            zz = j // nx
            xo = j % nx

            @pl.when(xo != x)
            def _():
                x_wait(h, xo, zz)

            for c in range(cap):
                gath[j * cap + c] = xr[h, xo, zz, :, c * BLK : (c + 1) * BLK, :]
            gkv[:, pl.ds(pl.multiple_of(j * GLEN, GLEN), GLEN), :] = xr[h, xo, zz, :, cap * BLK :, :]
            return 0

        lax.fori_loop(0, n, collect, 0)

        @pl.when(me > 0)
        def _():
            halo_copy(h, True).wait_recv()

        @pl.when(me < n - 1)
        def _():
            halo_copy(h, False).wait_recv()

        def window(blk):
            if blk < 0:
                return hr[h, 0]
            if blk >= nb:
                return hr[h, 1]
            return col[h, z, :, blk * BLK : (blk + 1) * BLK, :]

        wacc[h] = jnp.zeros_like(wacc[h])
        length = (3 + per) * BLK + n * GLEN
        column = lax.broadcasted_iota(jnp.int32, (BLK, length), 1)
        low = (3 + per) * BLK
        gsum_k = gsum_v = None
        for b in range(nb):
            parts = [window(b - 1), window(b), window(b + 1)]
            parts += [gath[place[b * per + r]] for r in range(per)]
            parts.append(gkv[...])
            kcat = jnp.concatenate([p[0] for p in parts], 0)
            vcat = jnp.concatenate([p[1] for p in parts], 0)
            at = slice(b * BLK, (b + 1) * BLK)
            q = q_ref[at, lanes(h)]
            g = g_ref[at, lanes(h)]
            s = dot(q, kcat, ((1,), (1,))) * scale
            if b == 0:
                s = jnp.where((column < BLK) & (me == 0), -jnp.inf, s)
            if b == nb - 1:
                s = jnp.where(
                    (column >= 2 * BLK) & (column < 3 * BLK) & (me == n - 1), -jnp.inf, s
                )
            e = jnp.exp(s - jnp.max(s, axis=1, keepdims=True))
            p = e * (1.0 / jnp.sum(e, axis=1, keepdims=True))
            pb = p.astype(BF16)
            o_ref[at, lanes(h)] = dot(pb, vcat, ((1,), (0,))).astype(BF16)
            dp = dot(g, vcat, ((1,), (1,)))
            delta = jnp.sum(p * dp, axis=1, keepdims=True)
            ds = (p * (dp - delta) * scale).astype(BF16)
            dq_ref[at, lanes(h)] = dot(ds, kcat, ((1,), (0,))).astype(BF16)
            dk = dot(ds, q, ((0,), (0,)))
            dv = dot(pb, g, ((0,), (0,)))
            for kv, term in ((0, dk), (1, dv)):
                wacc[h, kv, b * BLK : (b + 3) * BLK, :] += term[: 3 * BLK]
                for r in range(per):
                    tr[b * per + r, kv] = term[(3 + r) * BLK : (4 + r) * BLK].astype(BF16)
            gsum_k = dk[low:] if b == 0 else gsum_k + dk[low:]
            gsum_v = dv[low:] if b == 0 else gsum_v + dv[low:]
        gacc[0] = gsum_k.astype(BF16)
        gacc[1] = gsum_v.astype(BF16)

        def give(j, _):
            zz = j // nx
            xo = j % nx

            def put(dst):
                for c in range(cap):
                    dst[h, xo, zz, :, c * BLK : (c + 1) * BLK, :] = tr[inv[j * cap + c]]
                dst[h, xo, zz, :, cap * BLK :, :] = gacc[
                    :, pl.ds(pl.multiple_of(j * GLEN, GLEN), GLEN), :
                ]

            @pl.when(xo == x)
            def _():
                put(yr)

            @pl.when(xo != x)
            def _():
                x_copy(h, xo, zz).wait_send()
                put(xs)
                y_copy(h, xo, zz).start()

            return 0

        lax.fori_loop(0, n, give, 0)

        @pl.when(me > 0)
        def _():
            wh[h, 0] = wacc[h, :, 0:BLK, :].astype(BF16)
            w_copy(h, False).start()

        @pl.when(me < n - 1)
        def _():
            wh[h, 1] = wacc[h, :, rows + BLK :, :].astype(BF16)
            w_copy(h, True).start()

    def column_terms(h, zz):
        pieces = []
        slots = [
            (tgt[(d * nz + zz) * cap + c], yr[h, d, zz, :, c * BLK : (c + 1) * BLK, :].astype(F32))
            for d in range(nx)
            for c in range(cap)
        ]
        for blk in range(nb):
            total = None
            for target, term in slots:
                part = jnp.where(target == blk, term, 0.0)
                total = part if total is None else total + part
            pieces.append(total)
        total = None
        for d in range(nx):
            part = yr[h, d, zz, :, cap * BLK :, :].astype(F32)
            total = part if total is None else total + part
        return pieces, total

    def r_copy(h, zz, slot, up):
        return remote(
            rout.at[h, zz], rin.at[h, slot], r_send.at[h, zz], r_recv.at[h, slot],
            me + (nx if up else -nx),
        )

    def pass_on(h, zz, more):
        pieces, glob = column_terms(h, zz)

        def put(extra):
            for blk in range(nb):
                at = slice(blk * BLK, (blk + 1) * BLK)
                rout[h, zz, :, at, :] = extra(pieces[blk], at).astype(BF16)
            rout[h, zz, :, rows:ext, :] = extra(glob, slice(rows, ext)).astype(BF16)

        @pl.when(more)
        def _():
            r_copy(h, zz, zz, False).wait_recv()
            put(lambda v, at: v + rin[h, zz, :, at, :].astype(F32))

        @pl.when(jnp.logical_not(more))
        def _():
            put(lambda v, at: v)

    def pass_stage(h):
        def one(u, _):
            down = u - (nz - 1 - z)
            up = nz - 1 - (u - z)

            @pl.when((down >= 0) & (down < z))
            def _():
                pass_on(h, down, z < nz - 1)
                r_copy(h, down, down, False).start()

            @pl.when((up > z) & (up < nz))
            def _():
                pass_on(h, up, z > 0)

                @pl.when(up == z + 1)
                def _():
                    r_copy(h, up, nz, True).start()

                @pl.when(up != z + 1)
                def _():
                    r_copy(h, up, up, True).start()

            return 0

        lax.fori_loop(0, 2 * nz - 2, one, 0)

    def arrive_stage(h):
        def arrive(at, _):
            d = at // nz

            @pl.when(d != x)
            def _():
                y_wait(h, d, at % nz)

            return 0

        lax.fori_loop(0, nx * nz, arrive, 0)

    def final_stage(h):
        pieces, glob = column_terms(h, z)
        for blk in range(nb):
            at = slice(blk * BLK, (blk + 1) * BLK)
            wacc[h, :, BLK + blk * BLK : 2 * BLK + blk * BLK, :] += pieces[blk]

        @pl.when(me > 0)
        def _():
            w_copy(h, True).wait_recv()
            wacc[h, :, BLK : 2 * BLK, :] += wr[h, 1].astype(F32)

        @pl.when(me < n - 1)
        def _():
            w_copy(h, False).wait_recv()
            wacc[h, :, rows : rows + BLK, :] += wr[h, 0].astype(F32)

        @pl.when(z == nz - 1)
        def _():
            rin[h, z] = jnp.zeros_like(rin[h, z])

        @pl.when(z < nz - 1)
        def _():
            r_copy(h, z, z, False).wait_recv()

        @pl.when(z == 0)
        def _():
            rin[h, nz] = jnp.zeros_like(rin[h, nz])

        @pl.when(z > 0)
        def _():
            r_copy(h, z, nz, True).wait_recv()

        glob = glob + rin[h, z, :, rows:ext, :].astype(F32) + rin[h, nz, :, rows:ext, :].astype(F32)
        for blk in range(nb):
            at = slice(blk * BLK, (blk + 1) * BLK)
            total = (
                wacc[h, :, BLK + blk * BLK : 2 * BLK + blk * BLK, :]
                + rin[h, z, :, at, :].astype(F32)
                + rin[h, nz, :, at, :].astype(F32)
            )
            top = total[:, :GLEN] + jnp.where(own_global == blk, glob, 0.0)
            total = jnp.concatenate([top, total[:, GLEN:]], 1).astype(BF16)
            dk_ref[at, lanes(h)] = total[0]
            dv_ref[at, lanes(h)] = total[1]

    outer = (z == 0) | (z == nz - 1)

    def sums(h, mine):
        @pl.when((h >= 0) & (h < heads) & mine)
        def _():
            arrive_stage(h)
            pass_stage(h)

    def turn(i, _):
        t = i - (nz - 2)

        def half(part, _):
            @pl.when((part == 0) == outer)
            def _():
                sums(t - 2, True)

            @pl.when(part == 0)
            def _():
                gather_stage(t)

                @pl.when((t >= 1) & (t <= heads))
                def _():
                    compute_stage(t - 1)

            return 0

        lax.fori_loop(0, 2, half, 0)

        @pl.when(t >= 3)
        def _():
            final_stage(t - 3)

        return 0

    lax.fori_loop(0, heads + 3 + nz - 2, turn, 0)

    def drain(h, _):
        def shard(zz, _):
            @pl.when((zz <= z) & (z < nz - 1))
            def _():
                z_copy(h, zz, True).wait_send()

            @pl.when((zz >= z) & (z > 0))
            def _():
                z_copy(h, zz, False).wait_send()

            @pl.when(zz != z)
            def _():
                r_copy(h, zz, zz, False).wait_send()

            def partner(px, _):
                @pl.when(px != x)
                def _():
                    y_copy(h, px, zz).wait_send()

                return 0

            lax.fori_loop(0, nx, partner, 0)
            return 0

        lax.fori_loop(0, nz, shard, 0)

        @pl.when(me < n - 1)
        def _():
            halo_copy(h, True).wait_send()
            w_copy(h, True).wait_send()

        @pl.when(me > 0)
        def _():
            halo_copy(h, False).wait_send()
            w_copy(h, False).wait_send()

        return 0

    lax.fori_loop(0, heads, drain, 0)


def grid_of(n):
    nx = 1
    while nx * nx * 4 <= n and n % (nx * 2) == 0:
        nx *= 2
    return n // nx, nx


def shards(n, queries, keys, values, out_grad, rand_blocks, glob_blocks):
    rows, width = queries.shape
    heads = width // HDIM
    nb = rows // BLK
    per = rand_blocks.shape[1]
    spots = nb * per
    cap = max(2, (spots + n - 1) // n)
    nz, nx = grid_of(n)
    ext = rows + GLEN
    xrows = cap * BLK + GLEN
    out = jax.ShapeDtypeStruct((rows, width), BF16)
    vmem = pl.BlockSpec(memory_space=pltpu.VMEM)
    smem = pl.BlockSpec(memory_space=pltpu.SMEM)
    dma = pltpu.SemaphoreType.DMA
    slots = pltpu.VMEM((heads, nx, nz, 2, xrows, HDIM), BF16)
    edges = pltpu.VMEM((heads, 2, 2, BLK, HDIM), BF16)
    return pl.pallas_call(
        functools.partial(kernel, nz, nx, nb, per, cap, heads),
        out_shape=[out] * 4,
        in_specs=[smem, smem, vmem, vmem, vmem, vmem],
        out_specs=[vmem] * 4,
        scratch_shapes=[
            pltpu.VMEM((heads, nz, 2, ext, HDIM), BF16),
            slots, slots, slots,
            edges, edges, edges,
            pltpu.VMEM((heads, nz + 1, 2, ext, HDIM), BF16),
            pltpu.VMEM((heads, nz, 2, ext, HDIM), BF16),
            pltpu.VMEM((heads, 2, rows + 2 * BLK, HDIM), F32),
            pltpu.VMEM((n * cap, 2, BLK, HDIM), BF16),
            pltpu.VMEM((2, n * GLEN, HDIM), BF16),
            pltpu.VMEM((nb, 2, BLK, HDIM), BF16),
            pltpu.VMEM((spots + 1, 2, BLK, HDIM), BF16),
            pltpu.VMEM((2, n * GLEN, HDIM), BF16),
            pltpu.SMEM((nx * nz * cap,), jnp.int32),
            pltpu.SMEM((n * cap,), jnp.int32),
            pltpu.SMEM((spots,), jnp.int32),
            dma((heads, nz, 2)), dma((heads, nz)),
            dma((heads, nx, nz)), dma((heads, nx, nz)),
            dma((heads, nx, nz)), dma((heads, nx, nz)),
            dma((heads, 2)), dma((heads, 2)),
            dma((heads, 2)), dma((heads, 2)),
            dma((heads, nz)), dma((heads, nz + 1)),
        ],
        compiler_params=pltpu.CompilerParams(
            collective_id=0, has_side_effects=True, vmem_limit_bytes=60 * 1024 * 1024
        ),
    )(rand_blocks, glob_blocks, queries, keys, values, out_grad)


def solution(mesh):
    split = P("seq", "head")
    return jax.shard_map(
        functools.partial(shards, mesh.shape["seq"]),
        mesh=mesh,
        in_specs=(split, split, split, split, P(), P("seq")),
        out_specs=(split, split, split, split),
        check_vma=False,
    )
```

```python
import functools
import math

import jax
import jax.numpy as jnp
from jax import lax
from jax.experimental import pallas as pl
from jax.experimental.pallas import tpu as pltpu
from jax.sharding import PartitionSpec as P

HDIM = 128
BLK = 64
GLEN = 16
MESH = pl.DeviceIdType.MESH
F32 = jnp.float32
BF16 = jnp.bfloat16


def dot(a, b, dims):
    return lax.dot_general(a, b, (dims, ((), ())), preferred_element_type=F32)


def kernel(
    nz, nx, nb, per, cap, heads,
    rb_ref, gb_ref, q_ref, k_ref, v_ref, g_ref,
    o_ref, dq_ref, dk_ref, dv_ref,
    col, xs, xr, yr, hr, wh, wr, rin, rout, wacc, gath, gkv, tmp, tr, gacc,
    tgt, inv, place,
    z_send, z_recv, x_send, x_recv, y_send, y_recv, h_send, h_recv, w_send, w_recv, r_send, r_recv,
):
    n = nz * nx
    rows = nb * BLK
    spots = nb * per
    ext = rows + GLEN
    scale = 1.0 / math.sqrt(HDIM)
    lead = 2
    me = lax.axis_index("seq")
    z = me // nx
    x = me % nx

    def lanes(h):
        return pl.ds(pl.multiple_of(h * HDIM, HDIM), HDIM)

    def remote(src, dst, send, recv, dev):
        return pltpu.make_async_remote_copy(
            src_ref=src, dst_ref=dst, send_sem=send, recv_sem=recv,
            device_id={"seq": dev}, device_id_type=MESH,
        )

    barrier = pltpu.get_barrier_semaphore()
    for step in range(1, n):
        pl.semaphore_signal(
            barrier, inc=1, device_id={"seq": lax.rem(me + step, n)}, device_id_type=MESH
        )
    own_global = gb_ref[0] - me * nb

    def pack_own(h, _):
        for kv, ref in enumerate((k_ref, v_ref)):
            col[h, z, kv, 0:rows, :] = ref[:, lanes(h)]
            picked = ref[0:GLEN, lanes(h)]
            for blk in range(1, nb):
                at = slice(blk * BLK, blk * BLK + GLEN)
                picked = jnp.where(own_global == blk, ref[at, lanes(h)], picked)
            col[h, z, kv, rows:ext, :] = picked
        return 0

    lax.fori_loop(0, heads, pack_own, 0)
    pl.semaphore_wait(barrier, n - 1)

    def z_copy(h, zz, up):
        dev = me + (nx if up else -nx)
        return remote(
            col.at[h, zz], col.at[h, zz], z_send.at[h, zz, int(up)], z_recv.at[h, zz], dev
        )

    def halo_copy(h, nxt):
        edge = pl.ds(rows - BLK, BLK) if nxt else pl.ds(0, BLK)
        slot = 0 if nxt else 1
        return remote(
            col.at[h, z, :, edge, :], hr.at[h, slot],
            h_send.at[h, slot], h_recv.at[h, slot], me + (1 if nxt else -1),
        )

    def first_sends(h, _):
        @pl.when(z < nz - 1)
        def _():
            z_copy(h, z, True).start()

        @pl.when(z > 0)
        def _():
            z_copy(h, z, False).start()

        @pl.when(me < n - 1)
        def _():
            halo_copy(h, True).start()

        @pl.when(me > 0)
        def _():
            halo_copy(h, False).start()

        return 0

    lax.fori_loop(0, min(lead, heads), first_sends, 0)

    @pl.when(me == 0)
    def _():
        hr[:, 0] = jnp.zeros_like(hr[:, 0])

    @pl.when(me == n - 1)
    def _():
        hr[:, 1] = jnp.zeros_like(hr[:, 1])

    def own_entry(t):
        return rb_ref[me * nb + t // per, t % per]

    for t in range(spots):
        owner = lax.div(own_entry(t), nb)
        rank = jnp.int32(0)
        for s in range(t):
            rank = rank + (lax.div(own_entry(s), nb) == owner).astype(jnp.int32)
        place[t] = owner * cap + rank

    def fill_inv(j, _):
        count = jnp.int32(0)
        found = [jnp.int32(spots)] * cap
        for t in range(spots):
            hit = lax.div(own_entry(t), nb) == j
            for c in range(cap):
                found[c] = jnp.where(hit & (count == c), jnp.int32(t), found[c])
            count = count + hit.astype(jnp.int32)
        for c in range(cap):
            inv[j * cap + c] = found[c]
        return 0

    lax.fori_loop(0, n, fill_inv, 0)

    def fill_tgt(at, _):
        px = at // nz
        zz = at % nz
        j = zz * nx + x
        count = jnp.int32(0)
        found = [jnp.int32(-1)] * cap
        for t in range(spots):
            block = rb_ref[(z * nx + px) * nb + t // per, t % per]
            hit = lax.div(block, nb) == j
            for c in range(cap):
                found[c] = jnp.where(hit & (count == c), block - j * nb, found[c])
            count = count + hit.astype(jnp.int32)
        for c in range(cap):
            tgt[at * cap + c] = found[c]
        return 0

    lax.fori_loop(0, nx * nz, fill_tgt, 0)
    tr[spots] = jnp.zeros_like(tr[spots])

    def x_copy(h, px, zz):
        return remote(
            xs.at[h, px, zz], xr.at[h, x, zz], x_send.at[h, px, zz], x_recv.at[h, x, zz],
            z * nx + px,
        )

    def x_wait(h, xo, zz):
        remote(
            xs.at[h, xo, zz], xr.at[h, xo, zz], x_send.at[h, xo, zz], x_recv.at[h, xo, zz],
            z * nx + xo,
        ).wait_recv()

    def y_copy(h, xo, zz):
        return remote(
            xs.at[h, xo, zz], yr.at[h, x, zz], y_send.at[h, xo, zz], y_recv.at[h, x, zz],
            z * nx + xo,
        )

    def y_wait(h, d, zz):
        remote(
            xs.at[h, d, zz], yr.at[h, d, zz], y_send.at[h, d, zz], y_recv.at[h, d, zz],
            z * nx + d,
        ).wait_recv()

    def serve(h, zz):
        for blk in range(nb):
            tmp[blk] = col[h, zz, :, blk * BLK : (blk + 1) * BLK, :]

        def one(px, _):
            def put(dst):
                for c in range(cap):
                    block = jnp.maximum(tgt[(px * nz + zz) * cap + c], 0)
                    dst[h, px, zz, :, c * BLK : (c + 1) * BLK, :] = tmp[block]
                dst[h, px, zz, :, cap * BLK :, :] = col[h, zz, :, rows:ext, :]

            @pl.when(px == x)
            def _():
                put(xr)

            @pl.when(px != x)
            def _():
                put(xs)
                x_copy(h, px, zz).start()

            return 0

        lax.fori_loop(0, nx, one, 0)

    def gather_stage(t):
        def one(s, _):
            h = t + nz - 1 - s

            @pl.when((h >= 0) & (h < heads) & (s == 1))
            def _():
                @pl.when(h + lead < heads)
                def _():
                    first_sends(h + lead, 0)

                serve(h, z)

            @pl.when((h >= 0) & (h < heads) & (z - s >= 0))
            def _():
                zz = z - s
                z_copy(h, zz, True).wait_recv()

                @pl.when(z < nz - 1)
                def _():
                    z_copy(h, zz, True).start()

                serve(h, zz)

            @pl.when((h >= 0) & (h < heads) & (z + s < nz))
            def _():
                zz = z + s
                z_copy(h, zz, False).wait_recv()

                @pl.when(z > 0)
                def _():
                    z_copy(h, zz, False).start()

                serve(h, zz)

            return 0

        lax.fori_loop(1, nz, one, 0)

    def w_copy(h, nxt):
        slot = 1 if nxt else 0
        return remote(
            wh.at[h, slot], wr.at[h, slot], w_send.at[h, slot], w_recv.at[h, slot],
            me + (1 if nxt else -1),
        )

    def compute_stage(h):
        def collect(j, _):
            zz = j // nx
            xo = j % nx

            @pl.when(xo != x)
            def _():
                x_wait(h, xo, zz)

            for c in range(cap):
                gath[j * cap + c] = xr[h, xo, zz, :, c * BLK : (c + 1) * BLK, :]
            gkv[:, pl.ds(pl.multiple_of(j * GLEN, GLEN), GLEN), :] = xr[h, xo, zz, :, cap * BLK :, :]
            return 0

        lax.fori_loop(0, n, collect, 0)

        @pl.when(me > 0)
        def _():
            halo_copy(h, True).wait_recv()

        @pl.when(me < n - 1)
        def _():
            halo_copy(h, False).wait_recv()

        def window(blk):
            if blk < 0:
                return hr[h, 0]
            if blk >= nb:
                return hr[h, 1]
            return col[h, z, :, blk * BLK : (blk + 1) * BLK, :]

        wacc[h] = jnp.zeros_like(wacc[h])
        length = (3 + per) * BLK + n * GLEN
        column = lax.broadcasted_iota(jnp.int32, (BLK, length), 1)
        low = (3 + per) * BLK
        gsum_k = gsum_v = None
        for b in range(nb):
            parts = [window(b - 1), window(b), window(b + 1)]
            parts += [gath[place[b * per + r]] for r in range(per)]
            parts.append(gkv[...])
            kcat = jnp.concatenate([p[0] for p in parts], 0)
            vcat = jnp.concatenate([p[1] for p in parts], 0)
            at = slice(b * BLK, (b + 1) * BLK)
            q = q_ref[at, lanes(h)]
            g = g_ref[at, lanes(h)]
            s = dot(q, kcat, ((1,), (1,))) * scale
            if b == 0:
                s = jnp.where((column < BLK) & (me == 0), -jnp.inf, s)
            if b == nb - 1:
                s = jnp.where(
                    (column >= 2 * BLK) & (column < 3 * BLK) & (me == n - 1), -jnp.inf, s
                )
            e = jnp.exp(s - jnp.max(s, axis=1, keepdims=True))
            p = e * (1.0 / jnp.sum(e, axis=1, keepdims=True))
            pb = p.astype(BF16)
            o_ref[at, lanes(h)] = dot(pb, vcat, ((1,), (0,))).astype(BF16)
            dp = dot(g, vcat, ((1,), (1,)))
            delta = jnp.sum(p * dp, axis=1, keepdims=True)
            ds = (p * (dp - delta) * scale).astype(BF16)
            dq_ref[at, lanes(h)] = dot(ds, kcat, ((1,), (0,))).astype(BF16)
            dk = dot(ds, q, ((0,), (0,)))
            dv = dot(pb, g, ((0,), (0,)))
            for kv, term in ((0, dk), (1, dv)):
                wacc[h, kv, b * BLK : (b + 3) * BLK, :] += term[: 3 * BLK]
                for r in range(per):
                    tr[b * per + r, kv] = term[(3 + r) * BLK : (4 + r) * BLK].astype(BF16)
            gsum_k = dk[low:] if b == 0 else gsum_k + dk[low:]
            gsum_v = dv[low:] if b == 0 else gsum_v + dv[low:]
        gacc[0] = gsum_k.astype(BF16)
        gacc[1] = gsum_v.astype(BF16)

        def give(j, _):
            zz = j // nx
            xo = j % nx

            def put(dst):
                for c in range(cap):
                    dst[h, xo, zz, :, c * BLK : (c + 1) * BLK, :] = tr[inv[j * cap + c]]
                dst[h, xo, zz, :, cap * BLK :, :] = gacc[
                    :, pl.ds(pl.multiple_of(j * GLEN, GLEN), GLEN), :
                ]

            @pl.when(xo == x)
            def _():
                put(yr)

            @pl.when(xo != x)
            def _():
                x_copy(h, xo, zz).wait_send()
                put(xs)
                y_copy(h, xo, zz).start()

            return 0

        lax.fori_loop(0, n, give, 0)

        @pl.when(me > 0)
        def _():
            wh[h, 0] = wacc[h, :, 0:BLK, :].astype(BF16)
            w_copy(h, False).start()

        @pl.when(me < n - 1)
        def _():
            wh[h, 1] = wacc[h, :, rows + BLK :, :].astype(BF16)
            w_copy(h, True).start()

    def column_terms(h, zz):
        def arrive(d, _):
            @pl.when(d != x)
            def _():
                y_wait(h, d, zz)

            return 0

        lax.fori_loop(0, nx, arrive, 0)
        pieces = []
        slots = [
            (tgt[(d * nz + zz) * cap + c], yr[h, d, zz, :, c * BLK : (c + 1) * BLK, :].astype(F32))
            for d in range(nx)
            for c in range(cap)
        ]
        for blk in range(nb):
            total = None
            for target, term in slots:
                part = jnp.where(target == blk, term, 0.0)
                total = part if total is None else total + part
            pieces.append(total)
        total = None
        for d in range(nx):
            part = yr[h, d, zz, :, cap * BLK :, :].astype(F32)
            total = part if total is None else total + part
        return pieces, total

    def r_copy(h, zz, slot, up):
        return remote(
            rout.at[h, zz], rin.at[h, slot], r_send.at[h, zz], r_recv.at[h, slot],
            me + (nx if up else -nx),
        )

    def pass_on(h, zz, more):
        pieces, glob = column_terms(h, zz)

        def put(extra):
            for blk in range(nb):
                at = slice(blk * BLK, (blk + 1) * BLK)
                rout[h, zz, :, at, :] = extra(pieces[blk], at).astype(BF16)
            rout[h, zz, :, rows:ext, :] = extra(glob, slice(rows, ext)).astype(BF16)

        @pl.when(more)
        def _():
            r_copy(h, zz, zz, False).wait_recv()
            put(lambda v, at: v + rin[h, zz, :, at, :].astype(F32))

        @pl.when(jnp.logical_not(more))
        def _():
            put(lambda v, at: v)

    def pass_stage(h):
        def one(u, _):
            down = u - (nz - 1 - z)
            up = nz - 1 - (u - z)

            @pl.when((down >= 0) & (down < z))
            def _():
                pass_on(h, down, z < nz - 1)
                r_copy(h, down, down, False).start()

            @pl.when((up > z) & (up < nz))
            def _():
                pass_on(h, up, z > 0)

                @pl.when(up == z + 1)
                def _():
                    r_copy(h, up, nz, True).start()

                @pl.when(up != z + 1)
                def _():
                    r_copy(h, up, up, True).start()

            return 0

        lax.fori_loop(0, 2 * nz - 2, one, 0)

    def final_stage(h):
        pieces, glob = column_terms(h, z)
        for blk in range(nb):
            at = slice(blk * BLK, (blk + 1) * BLK)
            wacc[h, :, BLK + blk * BLK : 2 * BLK + blk * BLK, :] += pieces[blk]

        @pl.when(me > 0)
        def _():
            w_copy(h, True).wait_recv()
            wacc[h, :, BLK : 2 * BLK, :] += wr[h, 1].astype(F32)

        @pl.when(me < n - 1)
        def _():
            w_copy(h, False).wait_recv()
            wacc[h, :, rows : rows + BLK, :] += wr[h, 0].astype(F32)

        @pl.when(z == nz - 1)
        def _():
            rin[h, z] = jnp.zeros_like(rin[h, z])

        @pl.when(z < nz - 1)
        def _():
            r_copy(h, z, z, False).wait_recv()

        @pl.when(z == 0)
        def _():
            rin[h, nz] = jnp.zeros_like(rin[h, nz])

        @pl.when(z > 0)
        def _():
            r_copy(h, z, nz, True).wait_recv()

        glob = glob + rin[h, z, :, rows:ext, :].astype(F32) + rin[h, nz, :, rows:ext, :].astype(F32)
        for blk in range(nb):
            at = slice(blk * BLK, (blk + 1) * BLK)
            total = (
                wacc[h, :, BLK + blk * BLK : 2 * BLK + blk * BLK, :]
                + rin[h, z, :, at, :].astype(F32)
                + rin[h, nz, :, at, :].astype(F32)
            )
            top = total[:, :GLEN] + jnp.where(own_global == blk, glob, 0.0)
            total = jnp.concatenate([top, total[:, GLEN:]], 1).astype(BF16)
            dk_ref[at, lanes(h)] = total[0]
            dv_ref[at, lanes(h)] = total[1]

    outer = (z == 0) | (z == nz - 1)

    def sums(h, mine):
        @pl.when((h >= 0) & (h < heads) & mine)
        def _():
            pass_stage(h)

    def turn(i, _):
        t = i - (nz - 2)

        gather_stage(t)

        @pl.when((t >= 1) & (t <= heads))
        def _():
            compute_stage(t - 1)

        sums(t - 2, True)

        @pl.when(t >= 3)
        def _():
            final_stage(t - 3)

        return 0

    lax.fori_loop(0, heads + 3 + nz - 2, turn, 0)

    def drain(h, _):
        def shard(zz, _):
            @pl.when((zz <= z) & (z < nz - 1))
            def _():
                z_copy(h, zz, True).wait_send()

            @pl.when((zz >= z) & (z > 0))
            def _():
                z_copy(h, zz, False).wait_send()

            @pl.when(zz != z)
            def _():
                r_copy(h, zz, zz, False).wait_send()

            def partner(px, _):
                @pl.when(px != x)
                def _():
                    y_copy(h, px, zz).wait_send()

                return 0

            lax.fori_loop(0, nx, partner, 0)
            return 0

        lax.fori_loop(0, nz, shard, 0)

        @pl.when(me < n - 1)
        def _():
            halo_copy(h, True).wait_send()
            w_copy(h, True).wait_send()

        @pl.when(me > 0)
        def _():
            halo_copy(h, False).wait_send()
            w_copy(h, False).wait_send()

        return 0

    lax.fori_loop(0, heads, drain, 0)


def grid_of(n):
    nx = 1
    while nx * nx * 4 <= n and n % (nx * 2) == 0:
        nx *= 2
    return n // nx, nx


def shards(n, queries, keys, values, out_grad, rand_blocks, glob_blocks):
    rows, width = queries.shape
    heads = width // HDIM
    nb = rows // BLK
    per = rand_blocks.shape[1]
    spots = nb * per
    cap = max(2, (spots + n - 1) // n)
    nz, nx = grid_of(n)
    ext = rows + GLEN
    xrows = cap * BLK + GLEN
    out = jax.ShapeDtypeStruct((rows, width), BF16)
    vmem = pl.BlockSpec(memory_space=pltpu.VMEM)
    smem = pl.BlockSpec(memory_space=pltpu.SMEM)
    dma = pltpu.SemaphoreType.DMA
    slots = pltpu.VMEM((heads, nx, nz, 2, xrows, HDIM), BF16)
    edges = pltpu.VMEM((heads, 2, 2, BLK, HDIM), BF16)
    return pl.pallas_call(
        functools.partial(kernel, nz, nx, nb, per, cap, heads),
        out_shape=[out] * 4,
        in_specs=[smem, smem, vmem, vmem, vmem, vmem],
        out_specs=[vmem] * 4,
        scratch_shapes=[
            pltpu.VMEM((heads, nz, 2, ext, HDIM), BF16),
            slots, slots, slots,
            edges, edges, edges,
            pltpu.VMEM((heads, nz + 1, 2, ext, HDIM), BF16),
            pltpu.VMEM((heads, nz, 2, ext, HDIM), BF16),
            pltpu.VMEM((heads, 2, rows + 2 * BLK, HDIM), F32),
            pltpu.VMEM((n * cap, 2, BLK, HDIM), BF16),
            pltpu.VMEM((2, n * GLEN, HDIM), BF16),
            pltpu.VMEM((nb, 2, BLK, HDIM), BF16),
            pltpu.VMEM((spots + 1, 2, BLK, HDIM), BF16),
            pltpu.VMEM((2, n * GLEN, HDIM), BF16),
            pltpu.SMEM((nx * nz * cap,), jnp.int32),
            pltpu.SMEM((n * cap,), jnp.int32),
            pltpu.SMEM((spots,), jnp.int32),
            dma((heads, nz, 2)), dma((heads, nz)),
            dma((heads, nx, nz)), dma((heads, nx, nz)),
            dma((heads, nx, nz)), dma((heads, nx, nz)),
            dma((heads, 2)), dma((heads, 2)),
            dma((heads, 2)), dma((heads, 2)),
            dma((heads, nz)), dma((heads, nz + 1)),
        ],
        compiler_params=pltpu.CompilerParams(
            collective_id=0, has_side_effects=True, vmem_limit_bytes=60 * 1024 * 1024
        ),
    )(rand_blocks, glob_blocks, queries, keys, values, out_grad)


def solution(mesh):
    split = P("seq", "head")
    return jax.shard_map(
        functools.partial(shards, mesh.shape["seq"]),
        mesh=mesh,
        in_specs=(split, split, split, split, P(), P("seq")),
        out_specs=(split, split, split, split),
        check_vma=False,
    )
```
